32 devices in a mesh: row: 8 (over z, core), col: 4 (over y, x).
Axes of the slice: x: 2, y: 2, z: 4, core: 2. Of those that a mesh axis runs over, the one named last changes fastest.
Arguments:
- stiffness: bfloat16 [256, 16, 128, 128], P('row', 'col'), may hold values from -2.5 to 2.5
- stiff_columns: int32 [256, 16], P('row', 'col'), may hold values from 0 to 255, as said below
- stiff_stored: int32 [256, 16], P('row', 'col'), may hold values from 0 to 1, as said below
- prolongator: bfloat16 [256, 2, 128, 128], P(('row', 'col')), may hold values from -0.5 to 0.5
- prolong_columns: int32 [256, 2], replicated, may hold values from 0 to 31, as said below
Outputs:
- coarse_matrix: float32 [32, 32, 128, 128], P('row', 'col')
The draws below stay inside these ranges and needn't reach their ends.
Inputs may be any that keep to these rules, and one draw needn't show every extreme that they name: `stiff_columns`: slots q * 4 to q * 4 + 3 of every row name fine block columns q * 64 to (q + 1) * 64 - 1. `stiff_stored`: each row range of 32 rows has its own share of stored slots, and in every draw one such range has all of its slots stored. `prolong_columns`: column 0 is the aggregate of fine block row i; each aggregate holds exactly 8 fine block rows, all in one row range of 32 rows, and the aggregates of range q are q * 4 to q * 4 + 3; column 1 is another aggregate of the same range.
All inputs are finite; a program needn't handle non-finite values.
Results may differ from the reference program's by a relative error of at most 0.0029.
Values may be sent and summed in bfloat16 or wider, within the bound.
No kernel may reach another device: no remote copies, remote signals or barrier semaphores. Data moves between devices by JAX's collectives and lax.ppermute only.
A program may use at most 256 MiB of HBM per device.

```python
import math
import jax
import jax.numpy as jnp
from jax import lax

B = 128
AK = 4
PK = 2
G = 8
NF = 256
PANEL = 32
NCB = 32
N_COL = 4


def draw_stiff_columns(key, part):
    key = jax.random.fold_in(key, 11)
    range_width = NF // N_COL
    offset = jax.random.randint(key, (NF, N_COL * AK), 0, range_width)
    slot_group = jnp.arange(N_COL * AK, dtype=jnp.int32) // AK
    return (offset + slot_group[None, :] * range_width).astype(jnp.int32)


def draw_stiff_stored(key, part):
    key = jax.random.fold_in(key, 12)
    key_rates, key_picks, key_full = jax.random.split(key, 3)
    ranges_count = NF // PANEL
    exponents = jax.random.randint(key_rates, (ranges_count,), 0, 4)
    live_rates = jnp.left_shift(jnp.ones((ranges_count,), jnp.int32), exponents)
    full_range = jax.random.randint(key_full, (), 0, ranges_count)
    live_rates = jnp.where(jnp.arange(ranges_count, dtype=jnp.int32) == full_range, 8, live_rates)
    live_draws = jax.random.randint(key_picks, (ranges_count, PANEL, N_COL * AK), 0, 8)
    stored = (live_draws < live_rates[:, None, None]).astype(jnp.int32)
    return stored.reshape(NF, N_COL * AK)


def draw_prolong_columns(key, part):
    key = jax.random.fold_in(key, 13)
    key_order, key_other = jax.random.split(key)
    ranges_count = NF // PANEL
    agg_count = PANEL // G
    panel_keys = jax.random.split(key_order, ranges_count)
    shuffled = jax.vmap(lambda panel_key: jax.random.permutation(panel_key, PANEL))(panel_keys)
    own_aggregate = shuffled.astype(jnp.int32) // G
    shift_by = jax.random.randint(key_other, (ranges_count, PANEL), 1, agg_count)
    neighbour_aggregate = (own_aggregate + shift_by) % agg_count
    range_base = (jnp.arange(ranges_count, dtype=jnp.int32) * agg_count)[:, None]
    stacked = jnp.stack([own_aggregate + range_base, neighbour_aggregate + range_base], axis=-1)
    return stacked.reshape(NF, 2).astype(jnp.int32)


def steps_of(stream_key, shape, pieces, least, high):
    def one(axis_at, shards_of):
        heights = jax.random.uniform(jax.random.fold_in(jax.random.fold_in(stream_key, 6), axis_at), (shards_of,), jnp.float32, least / len(pieces), high / len(pieces))
        return jnp.repeat(jnp.exp(heights), shape[axis_at] // shards_of).reshape((-1,) + (1,) * (len(shape) - axis_at - 1))

    factor_of = one(*pieces[0])
    for cut in pieces[1:]:
        factor_of = factor_of * one(*cut)
    return factor_of


def normal_values(own_key, extent, scale, reach, cuts=(), kind=jnp.bfloat16):
    result = jax.random.normal(own_key, extent, jnp.float32) * scale
    if len(cuts) > 0:
        result = steps_of(own_key, extent, cuts, -0.22, 0.18) * result
    return jnp.clip(result, min=-reach, max=reach).astype(kind)


def setup_inputs(seed: int = 0) -> dict:
    key_of = jax.random.split(jax.random.key(seed), 6)
    return {
        "stiffness": normal_values(key_of[0], (NF, N_COL * AK, B, B), 0.3, 2.5, ((0, 8), (1, 4))),
        "stiff_columns": draw_stiff_columns(jax.random.fold_in(key_of[5], 71), 0),
        "stiff_stored": draw_stiff_stored(jax.random.fold_in(key_of[5], 71), 0),
        "prolongator": normal_values(key_of[3], (NF, PK, B, B), B ** -0.5, 0.5, ((0, 32),)),
        "prolong_columns": draw_prolong_columns(jax.random.fold_in(key_of[5], 71), 0),
    }


def reference(stiffness, stiff_columns, stiff_stored, prolongator, prolong_columns):
    block_size = stiffness.shape[2]
    row_step = math.gcd(NF, 16)
    segments = NCB * NCB

    def one_block(counter, coarse):
        first_row = (counter * row_step).astype(jnp.int32)
        stiff_rows = lax.dynamic_slice_in_dim(stiffness, first_row, row_step, 0).astype(jnp.float32)
        column_ids = lax.dynamic_slice_in_dim(stiff_columns, first_row, row_step, 0).astype(jnp.int32)
        live_mask = lax.dynamic_slice_in_dim(stiff_stored, first_row, row_step, 0).astype(jnp.float32)
        right_block = prolongator[column_ids].astype(jnp.float32)
        product = jnp.einsum("isxy,isbyz->isbxz", stiff_rows, right_block)
        product = (product * live_mask[:, :, None, None, None]).astype(jnp.bfloat16)
        product = lax.optimization_barrier(product).astype(jnp.float32)
        left_block = lax.dynamic_slice_in_dim(prolongator, first_row, row_step, 0).astype(jnp.float32)
        triple = jnp.einsum("iayx,isbyz->iasbxz", left_block, product)
        left_ids = lax.dynamic_slice_in_dim(prolong_columns, first_row, row_step, 0).astype(jnp.int32)
        right_ids = prolong_columns[column_ids].astype(jnp.int32)
        target_ids = left_ids[:, :, None, None] * NCB + right_ids[:, None, :, :]
        return coarse.at[target_ids.reshape(-1)].add(triple.reshape(-1, block_size, block_size))

    start_value = jnp.zeros((segments, block_size, block_size), jnp.float32)
    coarse = lax.fori_loop(jnp.int32(0), jnp.int32(NF // row_step), one_block, start_value)
    return coarse.reshape(NCB, NCB, block_size, block_size)
```

```python
import functools

import jax
import jax.numpy as jnp
from jax import lax
from jax.experimental import pallas as pl
from jax.experimental.pallas import tpu as pltpu
from jax.sharding import PartitionSpec as P

ACC_BYTES = 17 << 20
VMEM_LIMIT = 56 << 20


def left_kernel(group, col_ref, agg_ref, base_ref, *refs):
    *pieces, stiff_ref, out_ref, acc_ref = refs
    cols_count = out_ref.shape[0]
    slots = stiff_ref.shape[1]
    block = stiff_ref.shape[2]
    first_agg = pl.program_id(0) * group
    acc_ref[...] = jnp.zeros_like(acc_ref)

    for number, piece in enumerate(pieces):

        def one_row(j, carry, number=number, piece=piece):
            row = base_ref[number] + j
            left = jnp.concatenate([piece[j, 0].T, piece[j, 1].T], axis=0)
            for s in range(slots):
                col = col_ref[row * slots + s]
                terms = jnp.dot(left, stiff_ref[row, s], preferred_element_type=jnp.float32)
                for a in range(2):
                    agg = agg_ref[row * 2 + a] - first_agg
                    inside = jnp.logical_and(agg >= 0, agg < group)
                    at_col = jnp.where(inside, col, cols_count)
                    at_agg = jnp.where(inside, agg, 0)
                    acc_ref[at_col, at_agg] += terms[a * block : (a + 1) * block]
            return carry

        lax.fori_loop(0, piece.shape[0], one_row, 0)

    def one_col(k, carry):
        out_ref[k] = acc_ref[k].reshape(group * block, block).astype(jnp.bfloat16)
        return carry

    lax.fori_loop(0, cols_count, one_col, 0)


def left_sums(pieces, bases, stiffness, cols, aggs, cols_count, agg_rows):
    block = stiffness.shape[2]
    group = agg_rows
    while group > 1 and (cols_count + 1) * group * block * block * 4 > ACC_BYTES:
        group //= 2
    once = pl.Buffered(1)
    whole = lambda x: pl.BlockSpec(x.shape, lambda g, *_: (0,) * x.ndim, pipeline_mode=once)
    products = stiffness.shape[0] * stiffness.shape[1] * 2
    return pl.pallas_call(
        functools.partial(left_kernel, group),
        grid_spec=pltpu.PrefetchScalarGridSpec(
            num_scalar_prefetch=3,
            grid=(agg_rows // group,),
            in_specs=[whole(x) for x in (*pieces, stiffness)],
            out_specs=pl.BlockSpec(
                (cols_count, group * block, block), lambda g, *_: (0, g, 0), pipeline_mode=once
            ),
            scratch_shapes=[pltpu.VMEM((cols_count + 1, group, block, block), jnp.float32)],
        ),
        out_shape=jax.ShapeDtypeStruct((cols_count, agg_rows * block, block), jnp.bfloat16),
        compiler_params=pltpu.CompilerParams(vmem_limit_bytes=VMEM_LIMIT),
        cost_estimate=pl.CostEstimate(
            flops=4 * products * block**3, bytes_accessed=16 << 20, transcendentals=0
        ),
        name="left_sums",
    )(cols, aggs, bases, *pieces, stiffness)


def right_kernel(count, first, agg_ref, chunk_ref, *refs):
    sums, pieces = refs[:count], refs[count : 2 * count]
    out_ref = refs[-1]
    aggs, block = out_ref.shape[0], out_ref.shape[2]
    per = pieces[0].shape[0]
    if first:
        out_ref[...] = jnp.zeros_like(out_ref)
    else:
        out_ref[...] = refs[2 * count][...]
    for number in range(count):

        def one_row(j, carry, number=number):
            row = chunk_ref[number] * per + j
            right = jnp.concatenate([pieces[number][j, 0], pieces[number][j, 1]], axis=1)
            terms = jnp.dot(sums[number][j], right, preferred_element_type=jnp.float32)
            for b in range(2):
                agg = agg_ref[row * 2 + b]
                part = terms[:, b * block : (b + 1) * block].reshape(aggs, block, block)
                out_ref[:, agg] += part
            return carry

        lax.fori_loop(0, per, one_row, 0)


def right_sums(sums, pieces, chunks, aggs, before, shape):
    count = len(pieces)
    per, block = pieces[0].shape[0], pieces[0].shape[2]
    once = pl.Buffered(1)
    whole = lambda x: pl.BlockSpec(x.shape, lambda g, *_: (0,) * x.ndim, pipeline_mode=once)
    out = jax.ShapeDtypeStruct(shape, jnp.float32)
    rest = () if before is None else (before,)
    return pl.pallas_call(
        functools.partial(right_kernel, count, before is None),
        grid_spec=pltpu.PrefetchScalarGridSpec(
            num_scalar_prefetch=2,
            grid=(1,),
            in_specs=[
                pl.BlockSpec(
                    (per,) + sums.shape[1:],
                    lambda g, agg, chunk, n=n: (chunk[n], 0, 0),
                    pipeline_mode=once,
                )
                for n in range(count)
            ]
            + [whole(x) for x in (*pieces, *rest)],
            out_specs=whole(out),
        ),
        out_shape=out,
        input_output_aliases={} if before is None else {2 + 2 * count: 0},
        compiler_params=pltpu.CompilerParams(vmem_limit_bytes=VMEM_LIMIT),
        cost_estimate=pl.CostEstimate(
            flops=4 * count * per * sums.shape[1] * block**2,
            bytes_accessed=(4 << 20) + count * (2 << 20),
            transcendentals=0,
        ),
        name="right_sums",
    )(aggs, chunks, *([sums] * count), *pieces, *rest)


def shards(stiffness, stiff_columns, stiff_stored, prolongator, prolong_columns):
    rows_count, block = stiffness.shape[0], stiffness.shape[2]
    per = prolongator.shape[0]
    row_count, col_count = lax.axis_size("row"), lax.axis_size("col")
    ratio = row_count // col_count
    row_pos, col_pos = lax.axis_index("row"), lax.axis_index("col")
    range_pos, member = row_pos // ratio, row_pos % ratio
    agg_rows = rows_count // 8
    agg_cols = ratio * agg_rows
    cols_count = ratio * rows_count
    first_fine = col_pos * cols_count

    def across(x, d):
        return lax.ppermute(x, "col", [(c, c ^ d) for c in range(col_count)])

    def fetch(x, m):
        pairs = [
            ((c * ratio + k) * col_count + (q ^ c ^ m), (q * ratio + k) * col_count + c)
            for q in range(col_count)
            for k in range(ratio)
            for c in range(col_count)
        ]
        return lax.ppermute(x, ("row", "col"), pairs)

    def beside(x, j):
        return lax.ppermute(
            x, "row", [(r, r // ratio * ratio + (r + j) % ratio) for r in range(row_count)]
        )

    right = {}
    own = prolongator
    order = list(range(col_count))
    if col_count == 4:
        order = [0, 3, 1, 2]
    near = [d for d in range(1, col_count) if d & (d - 1) == 0]
    pieces = [(own, 0, 0)] + [(across(own, d), d, 0) for d in near]
    for m in order[: col_count // 2]:
        right[m] = fetch(own, m)
    later, *held = lax.optimization_barrier((own, *[x for x, _, _ in pieces[1:]]))
    pieces[1:] = [(x, d, s) for x, (_, d, s) in zip(held, pieces[1:])]
    half = per // 2
    for d in range(1, col_count):
        if d in near:
            continue
        low = d & -d
        if d & (d - 1) == low or (d ^ low) in near:
            high = d ^ low
            by = {x_d: x for x, x_d, _ in pieces}
            pieces.append((across(by[high][:half], low), d, 0))
            pieces.append((across(by[low][half:], high), d, half))
        else:
            pieces.append((across(later, d), d, 0))
    for m in order[col_count // 2 :]:
        right[m] = fetch(later, m)

    cols = jnp.where(stiff_stored != 0, stiff_columns - first_fine, cols_count).reshape(-1)
    left_aggs = (
        lax.dynamic_slice_in_dim(prolong_columns, row_pos * rows_count, rows_count, 0)
        - row_pos * agg_rows
    ).reshape(-1)
    right_aggs = (
        lax.dynamic_slice_in_dim(prolong_columns, first_fine, cols_count, 0) - col_pos * agg_cols
    ).reshape(-1)
    bases = jnp.stack([(col_pos ^ d) * per + s for _, d, s in pieces]).astype(jnp.int32)

    sums = left_sums(
        [x for x, _, _ in pieces], bases, stiffness, cols, left_aggs, cols_count, agg_rows
    )

    shape = (agg_rows, agg_cols, block, block)
    coarse = None
    for part in (order[: col_count // 2], order[col_count // 2 :]):
        arrays, chunks = [], []
        for m in part:
            for j in range(ratio):
                arrays.append(right[m] if j == 0 else beside(right[m], j))
                panel = (member - j) % ratio
                chunks.append(panel * col_count + (range_pos ^ col_pos ^ m))
        chunks = jnp.stack(chunks).astype(jnp.int32)
        coarse = right_sums(sums, arrays, chunks, right_aggs, coarse, shape)
    return coarse


def solution(mesh):
    return jax.shard_map(
        shards,
        mesh=mesh,
        in_specs=(
            P("row", "col", None, None),
            P("row", "col"),
            P("row", "col"),
            P(("row", "col"), None, None, None),
            P(),
        ),
        out_specs=P("row", "col", None, None),
        check_vma=False,
    )
```

```python
import functools

import jax
import jax.numpy as jnp
from jax import lax
from jax.experimental import pallas as pl
from jax.experimental.pallas import tpu as pltpu
from jax.sharding import PartitionSpec as P

G = 8
UNIT = 8
VMEM_LIMIT = 16 << 20
HBM = pl.BlockSpec(memory_space=pltpu.HBM)
SMEM = pl.BlockSpec(memory_space=pltpu.SMEM)
VMEM = pl.BlockSpec(memory_space=pltpu.VMEM)
ROW_BITS, AGG_BITS = 8, 5


def in_vmem(x):
    return pltpu.with_memory_space_constraint(x, pltpu.VMEM)


def in_hbm(x):
    return pltpu.with_memory_space_constraint(x, pltpu.HBM)


class Sizes:
    def __init__(self, stiffness, prolongator, row_count, col_count):
        self.rows, self.slots, self.block = stiffness.shape[:3]
        self.per = prolongator.shape[0]
        self.row_count, self.col_count = row_count, col_count
        self.ratio = row_count // col_count
        self.agg_rows = self.rows // G
        self.agg_cols = self.ratio * self.agg_rows
        self.cols = self.ratio * self.rows
        self.chunks = self.cols // self.per
        self.slots_count = self.rows * self.slots
        order = [0, 3, 1, 2] if col_count == 4 else list(range(col_count))
        self.early, self.late = order[: col_count // 2], order[col_count // 2 :]
        members = range(self.ratio)
        self.batches = [
            [(m, j) for m in self.early for j in members],
            [(m, 0) for m in self.late],
            [(m, j) for m in self.late for j in members if j],
        ]
        spare = len(self.batches) * (UNIT - 1)
        self.units = -(-(self.slots_count + spare) // UNIT)
        self.entries = self.units * UNIT
        self.place_at = 0
        self.start_at = self.slots_count
        self.entry_at = self.start_at + len(self.batches) + 1
        self.table = self.entry_at + self.entries
        self.per_bits = self.per.bit_length() - 1
        assert self.per == 1 << self.per_bits
        assert self.chunks * self.per <= 1 << ROW_BITS
        assert max(self.agg_rows, self.agg_cols) < 1 << AGG_BITS
        block = self.block
        self.terms_shape = (self.entries + 1, 2 * block, block)
        self.acc_shape = ((self.agg_rows + 1) * self.agg_cols, block, block)


def position(z):
    row_pos, col_pos = lax.axis_index("row"), lax.axis_index("col")
    return row_pos, col_pos, row_pos // z.ratio, row_pos % z.ratio


def list_slots(z, columns_ref, stored_ref, prolong_ref, table_ref, fill_ref, batch_ref, base_ref):
    row_pos, col_pos, range_pos, member = position(z)
    first_fine = col_pos * z.cols
    first_row = row_pos * z.rows
    first_agg = row_pos * z.agg_rows
    first_agg_col = col_pos * z.agg_cols
    right_shift = ROW_BITS + 2 * AGG_BITS
    padding = z.agg_rows * ((1 << ROW_BITS) + (1 << (ROW_BITS + AGG_BITS)))

    for b, batch in enumerate(z.batches):
        fill_ref[b] = 0
        for at, (m, j) in enumerate(batch):
            panel = lax.rem(member - j + z.ratio, z.ratio)
            chunk = panel * z.col_count + (range_pos ^ col_pos ^ m)
            batch_ref[chunk] = b
            base_ref[chunk] = at * z.per

    def count(i, carry):
        for s in range(z.slots):
            chunk = lax.shift_right_logical(columns_ref[s, i] - first_fine, z.per_bits)
            b = batch_ref[chunk]
            fill_ref[b] += jnp.where(stored_ref[s, i] != 0, 1, 0)
        return carry

    lax.fori_loop(0, z.rows, count, 0)

    at = 0
    for b in range(len(z.batches)):
        table_ref[z.start_at + b] = at
        after = at + (fill_ref[b] + (UNIT - 1)) // UNIT * UNIT
        fill_ref[b] = at

        @pl.when(after > at)
        def _(after=after):
            for u in range(1, UNIT):
                table_ref[z.entry_at + after - u] = padding

        at = after
    table_ref[z.start_at + len(z.batches)] = at

    def place(i, carry):
        first = prolong_ref[0, first_row + i] - first_agg
        second = prolong_ref[1, first_row + i] - first_agg
        left = first * (1 << ROW_BITS) + second * (1 << (ROW_BITS + AGG_BITS))
        for s in range(z.slots):
            column = columns_ref[s, i]
            col = column - first_fine
            chunk = lax.shift_right_logical(col, z.per_bits)
            b = batch_ref[chunk]
            row = base_ref[chunk] + (col & (z.per - 1))
            right = (prolong_ref[0, column] - first_agg_col) * (1 << right_shift)
            right += (prolong_ref[1, column] - first_agg_col) * (1 << (right_shift + AGG_BITS))
            stored = stored_ref[s, i] != 0
            at = fill_ref[b]
            table_ref[z.place_at + i * z.slots + s] = jnp.where(stored, at, z.entries)

            @pl.when(stored)
            def _(b=b, at=at, entry=row + left + right):
                table_ref[z.entry_at + at] = entry
                fill_ref[b] = at + 1

        return carry

    lax.fori_loop(0, z.rows, place, 0)


def left_rows(z, chunk, parts, table_ref, stiff_ref, terms_ref):
    first = chunk * z.per
    row = 0
    for piece in parts:
        for j in range(piece.shape[0]):
            left = jnp.concatenate([piece[j, 0].T, piece[j, 1].T], axis=0)
            for s in range(0, z.slots, 2):
                pair = range(s, min(s + 2, z.slots))
                right = jnp.concatenate([stiff_ref[first + row, t] for t in pair], axis=1)
                terms = jnp.dot(left, right, preferred_element_type=jnp.float32)
                for at, t in enumerate(pair):
                    place = table_ref[z.place_at + (first + row) * z.slots + t]
                    terms_ref[place] = terms[:, at * z.block : (at + 1) * z.block].astype(
                        jnp.bfloat16
                    )
            row += 1


def first_kernel(z, columns_ref, stored_ref, prolong_ref, stiff_ref, own_ref, *refs):
    table_ref, held_ref, terms_ref, acc_ref, *scratch, sem = refs
    col_pos = lax.axis_index("col")
    load = pltpu.make_async_copy(stiff_ref, held_ref, sem)
    load.start()
    list_slots(z, columns_ref, stored_ref, prolong_ref, table_ref, *scratch)
    acc_ref[...] = jnp.zeros_like(acc_ref)
    load.wait()
    left_rows(z, col_pos, [own_ref], table_ref, held_ref, terms_ref)


def first_step(z, columns, stored, prolong_columns, stiffness, own):
    return pl.pallas_call(
        functools.partial(first_kernel, z),
        in_specs=[SMEM] * 3 + [HBM, VMEM],
        out_specs=[SMEM, VMEM, VMEM, VMEM],
        out_shape=[
            jax.ShapeDtypeStruct((z.table,), jnp.int32),
            pltpu.VMEM(stiffness.shape, stiffness.dtype),
            pltpu.VMEM(z.terms_shape, jnp.bfloat16),
            pltpu.VMEM(z.acc_shape, jnp.float32),
        ],
        scratch_shapes=[
            pltpu.SMEM((len(z.batches),), jnp.int32),
            pltpu.SMEM((z.chunks,), jnp.int32),
            pltpu.SMEM((z.chunks,), jnp.int32),
            pltpu.SemaphoreType.DMA,
        ],
        compiler_params=pltpu.CompilerParams(vmem_limit_bytes=VMEM_LIMIT),
        cost_estimate=pl.CostEstimate(
            flops=1 << 33, bytes_accessed=64 << 20, transcendentals=0
        ),
        name="first_step",
    )(columns.T, stored.T, prolong_columns.T, in_hbm(stiffness), own)


def left_kernel(z, groups, table_ref, held_ref, *refs):
    terms_ref = refs[-1]
    col_pos = lax.axis_index("col")
    taken = 0
    for d, count in groups:
        left_rows(z, col_pos ^ d, refs[taken : taken + count], table_ref, held_ref, terms_ref)
        taken += count


def left_terms(z, groups, table, held, terms):
    pieces = [x for _, parts in groups for x in parts]
    n = len(groups)
    return pl.pallas_call(
        functools.partial(left_kernel, z, [(d, len(parts)) for d, parts in groups]),
        in_specs=[SMEM, VMEM] + [VMEM] * len(pieces) + [VMEM],
        out_specs=VMEM,
        out_shape=pltpu.VMEM(z.terms_shape, jnp.bfloat16),
        input_output_aliases={2 + len(pieces): 0},
        compiler_params=pltpu.CompilerParams(vmem_limit_bytes=VMEM_LIMIT),
        cost_estimate=pl.CostEstimate(
            flops=n << 32, bytes_accessed=n * (32 << 20), transcendentals=0
        ),
        name="left_terms",
    )(table, in_vmem(held), *pieces, in_vmem(terms))


def right_kernel(z, number, last, table_ref, terms_ref, *refs):
    count = len(z.batches[number])
    pieces = refs[:count]
    out_ref, right_ref, sem = refs[count + 1 :]
    acc_ref = refs[count] if last else out_ref
    copies = []
    for at, piece in enumerate(pieces):
        copy = pltpu.make_async_copy(piece, right_ref.at[pl.ds(at * z.per, z.per)], sem.at[at])
        copy.start()
        copies.append(copy)
    for copy in copies:
        copy.wait()

    def field(entry, shift):
        return lax.shift_right_logical(entry, shift) & ((1 << AGG_BITS) - 1)

    def one_unit(unit, carry):
        parts = []
        for u in range(UNIT):
            entry = table_ref[z.entry_at + unit * UNIT + u]
            row = entry & ((1 << ROW_BITS) - 1)
            right = jnp.concatenate([right_ref[row, 0], right_ref[row, 1]], axis=1)
            value = jnp.dot(terms_ref[unit * UNIT + u], right, preferred_element_type=jnp.float32)
            aggs = [field(entry, ROW_BITS + n * AGG_BITS) for n in range(4)]
            parts.append((aggs, value))
        for aggs, value in parts:
            for a in range(2):
                for b in range(2):
                    acc_ref[aggs[a] * z.agg_cols + aggs[2 + b]] += value[
                        a * z.block : (a + 1) * z.block, b * z.block : (b + 1) * z.block
                    ]
        return carry

    begin = table_ref[z.start_at + number] // UNIT
    end = table_ref[z.start_at + number + 1] // UNIT
    lax.fori_loop(begin, end, one_unit, 0)
    if last:
        copy = pltpu.make_async_copy(
            acc_ref.at[pl.ds(0, z.agg_rows * z.agg_cols)], out_ref, sem.at[0]
        )
        copy.start()
        copy.wait()


def right_sums(z, number, pieces, table, terms, acc):
    count = len(pieces)
    last = number == len(z.batches) - 1
    if last:
        out_shape = jax.ShapeDtypeStruct(
            (z.agg_rows * z.agg_cols, z.block, z.block), jnp.float32
        )
    else:
        out_shape = pltpu.VMEM(z.acc_shape, jnp.float32)
    return pl.pallas_call(
        functools.partial(right_kernel, z, number, last),
        in_specs=[SMEM, VMEM] + [HBM] * count + [VMEM],
        out_specs=HBM if last else VMEM,
        out_shape=out_shape,
        scratch_shapes=[
            pltpu.VMEM((count * z.per, 2, z.block, z.block), jnp.bfloat16),
            pltpu.SemaphoreType.DMA((count,)),
        ],
        input_output_aliases={} if last else {2 + count: 0},
        compiler_params=pltpu.CompilerParams(vmem_limit_bytes=VMEM_LIMIT),
        cost_estimate=pl.CostEstimate(
            flops=count << 32, bytes_accessed=count * (32 << 20), transcendentals=0
        ),
        name="right_sums",
    )(table, in_vmem(terms), *pieces, in_vmem(acc))


def shards(stiffness, stiff_columns, stiff_stored, prolongator, prolong_columns):
    z = Sizes(stiffness, prolongator, lax.axis_size("row"), lax.axis_size("col"))
    bar = lax.optimization_barrier

    def across(x, d):
        return lax.ppermute(x, "col", [(c, c ^ d) for c in range(z.col_count)])

    def fetch(x, m):
        pairs = [
            ((c * z.ratio + k) * z.col_count + (q ^ c ^ m), (q * z.ratio + k) * z.col_count + c)
            for q in range(z.col_count)
            for k in range(z.ratio)
            for c in range(z.col_count)
        ]
        return lax.ppermute(x, ("row", "col"), pairs)

    def beside(x, j):
        return lax.ppermute(
            x, "row", [(r, r // z.ratio * z.ratio + (r + j) % z.ratio) for r in range(z.row_count)]
        )

    near = [d for d in range(1, z.col_count) if d & (d - 1) == 0]
    held = [across(prolongator, d) for d in near]
    right = {(m, 0): fetch(prolongator, m) for m in z.early}
    table, stiff, terms, acc = first_step(
        z, stiff_columns, stiff_stored, prolong_columns, stiffness, prolongator
    )
    table, *held = bar((table, *held))
    by = dict(zip(near, held))
    half = z.per // 2
    far = []
    for d in range(1, z.col_count):
        low = d & -d
        if d == low:
            continue
        if d ^ low in near:
            high = d ^ low
            far.append((d, [across(by[high][:half], low), across(by[low][half:], high)]))
        else:
            far.append((d, [across(prolongator, d)]))
    terms = left_terms(z, [(d, [by[d]]) for d in near], table, stiff, terms)
    again, table, *held = bar((prolongator, table, *right.values()))
    right = dict(zip(right, held))
    right |= {(m, 0): fetch(again, m) for m in z.late}
    others = range(1, z.ratio)
    right |= {(m, j): beside(right[m, 0], j) for m in z.early for j in others}
    terms = left_terms(z, far, table, stiff, terms)
    acc = right_sums(z, 0, [right[p] for p in z.batches[0]], table, terms, acc)
    table, *held = bar((table, *[right[m, 0] for m in z.late]))
    right |= {(m, 0): x for m, x in zip(z.late, held)}
    right |= {(m, j): beside(right[m, 0], j) for m in z.late for j in others}
    acc = right_sums(z, 1, [right[p] for p in z.batches[1]], table, terms, acc)
    coarse = right_sums(z, 2, [right[p] for p in z.batches[2]], table, terms, acc)
    return coarse.reshape(z.agg_rows, z.agg_cols, z.block, z.block)


def solution(mesh):
    return jax.shard_map(
        shards,
        mesh=mesh,
        in_specs=(
            P("row", "col", None, None),
            P("row", "col"),
            P("row", "col"),
            P(("row", "col"), None, None, None),
            P(),
        ),
        out_specs=P("row", "col", None, None),
        check_vma=False,
    )
```

```python
import functools

import jax
import jax.numpy as jnp
from jax import lax
from jax.experimental import pallas as pl
from jax.experimental.pallas import tpu as pltpu
from jax.sharding import PartitionSpec as P

G = 8
UNIT = 16
VMEM_LIMIT = 16 << 20
HBM = pl.BlockSpec(memory_space=pltpu.HBM)
SMEM = pl.BlockSpec(memory_space=pltpu.SMEM)
VMEM = pl.BlockSpec(memory_space=pltpu.VMEM)
ROW_BITS, AGG_BITS = 8, 5


def in_vmem(x):
    return pltpu.with_memory_space_constraint(x, pltpu.VMEM)


def in_hbm(x):
    return pltpu.with_memory_space_constraint(x, pltpu.HBM)


class Sizes:
    def __init__(self, stiffness, prolongator, row_count, col_count):
        self.rows, self.slots, self.block = stiffness.shape[:3]
        self.per = prolongator.shape[0]
        self.row_count, self.col_count = row_count, col_count
        self.ratio = row_count // col_count
        self.agg_rows = self.rows // G
        self.agg_cols = self.ratio * self.agg_rows
        self.cols = self.ratio * self.rows
        self.chunks = self.cols // self.per
        self.slots_count = self.rows * self.slots
        order = [0, 3, 1, 2] if col_count == 4 else list(range(col_count))
        self.early, self.late = order[: col_count // 2], order[col_count // 2 :]
        members = range(self.ratio)
        self.batches = [
            [(m, j) for m in self.early for j in members],
            [(m, 0) for m in self.late],
            [(m, j) for m in self.late for j in members if j],
        ]
        spare = len(self.batches) * (UNIT - 1)
        self.units = -(-(self.slots_count + spare) // UNIT)
        self.entries = self.units * UNIT
        self.place_at = 0
        self.start_at = self.slots_count
        self.entry_at = self.start_at + len(self.batches) + 1
        self.table = self.entry_at + self.entries
        self.per_bits = self.per.bit_length() - 1
        assert self.per == 1 << self.per_bits
        assert self.chunks * self.per <= 1 << ROW_BITS
        assert max(self.agg_rows, self.agg_cols) < 1 << AGG_BITS
        block = self.block
        self.terms_shape = (self.entries + 1, 2 * block, block)
        self.acc_shape = ((self.agg_rows + 1) * self.agg_cols, block, block)


def position(z):
    row_pos, col_pos = lax.axis_index("row"), lax.axis_index("col")
    return row_pos, col_pos, row_pos // z.ratio, row_pos % z.ratio


def list_slots(z, columns_ref, stored_ref, prolong_ref, table_ref, fill_ref, batch_ref, base_ref):
    row_pos, col_pos, range_pos, member = position(z)
    first_fine = col_pos * z.cols
    first_row = row_pos * z.rows
    first_agg = row_pos * z.agg_rows
    first_agg_col = col_pos * z.agg_cols
    right_shift = ROW_BITS + 2 * AGG_BITS
    padding = z.agg_rows * ((1 << ROW_BITS) + (1 << (ROW_BITS + AGG_BITS)))

    for b, batch in enumerate(z.batches):
        fill_ref[b] = 0
        for at, (m, j) in enumerate(batch):
            panel = lax.rem(member - j + z.ratio, z.ratio)
            chunk = panel * z.col_count + (range_pos ^ col_pos ^ m)
            batch_ref[chunk] = b
            base_ref[chunk] = at * z.per

    def count(i, carry):
        for s in range(z.slots):
            chunk = lax.shift_right_logical(columns_ref[s, i] - first_fine, z.per_bits)
            b = batch_ref[chunk]
            fill_ref[b] += jnp.where(stored_ref[s, i] != 0, 1, 0)
        return carry

    lax.fori_loop(0, z.rows, count, 0)

    at = 0
    for b in range(len(z.batches)):
        table_ref[z.start_at + b] = at
        after = at + (fill_ref[b] + (UNIT - 1)) // UNIT * UNIT
        fill_ref[b] = at

        @pl.when(after > at)
        def _(after=after):
            for u in range(1, UNIT):
                table_ref[z.entry_at + after - u] = padding

        at = after
    table_ref[z.start_at + len(z.batches)] = at

    def place(i, carry):
        first = prolong_ref[0, first_row + i] - first_agg
        second = prolong_ref[1, first_row + i] - first_agg
        left = first * (1 << ROW_BITS) + second * (1 << (ROW_BITS + AGG_BITS))
        for s in range(z.slots):
            column = columns_ref[s, i]
            col = column - first_fine
            chunk = lax.shift_right_logical(col, z.per_bits)
            b = batch_ref[chunk]
            row = base_ref[chunk] + (col & (z.per - 1))
            right = (prolong_ref[0, column] - first_agg_col) * (1 << right_shift)
            right += (prolong_ref[1, column] - first_agg_col) * (1 << (right_shift + AGG_BITS))
            stored = stored_ref[s, i] != 0
            at = fill_ref[b]
            table_ref[z.place_at + i * z.slots + s] = jnp.where(stored, at, z.entries)

            @pl.when(stored)
            def _(b=b, at=at, entry=row + left + right):
                table_ref[z.entry_at + at] = entry
                fill_ref[b] = at + 1

        return carry

    lax.fori_loop(0, z.rows, place, 0)


def left_rows(z, chunk, parts, table_ref, stiff_ref, terms_ref):
    first = chunk * z.per
    row = 0
    for piece in parts:
        for j in range(piece.shape[0]):
            left = jnp.concatenate([piece[j, 0].T, piece[j, 1].T], axis=0)
            for s in range(0, z.slots, 2):
                pair = range(s, min(s + 2, z.slots))
                right = jnp.concatenate([stiff_ref[first + row, t] for t in pair], axis=1)
                terms = jnp.dot(left, right, preferred_element_type=jnp.float32)
                for at, t in enumerate(pair):
                    place = table_ref[z.place_at + (first + row) * z.slots + t]
                    terms_ref[place] = terms[:, at * z.block : (at + 1) * z.block].astype(
                        jnp.bfloat16
                    )
            row += 1


def first_kernel(z, columns_ref, stored_ref, prolong_ref, stiff_ref, own_ref, *refs):
    table_ref, held_ref, terms_ref, acc_ref, *scratch, sem = refs
    col_pos = lax.axis_index("col")
    load = pltpu.make_async_copy(stiff_ref, held_ref, sem)
    load.start()
    list_slots(z, columns_ref, stored_ref, prolong_ref, table_ref, *scratch)
    acc_ref[...] = jnp.zeros_like(acc_ref)
    load.wait()
    left_rows(z, col_pos, [own_ref], table_ref, held_ref, terms_ref)


def first_step(z, columns, stored, prolong_columns, stiffness, own):
    return pl.pallas_call(
        functools.partial(first_kernel, z),
        in_specs=[SMEM] * 3 + [HBM, VMEM],
        out_specs=[SMEM, VMEM, VMEM, VMEM],
        out_shape=[
            jax.ShapeDtypeStruct((z.table,), jnp.int32),
            pltpu.VMEM(stiffness.shape, stiffness.dtype),
            pltpu.VMEM(z.terms_shape, jnp.bfloat16),
            pltpu.VMEM(z.acc_shape, jnp.float32),
        ],
        scratch_shapes=[
            pltpu.SMEM((len(z.batches),), jnp.int32),
            pltpu.SMEM((z.chunks,), jnp.int32),
            pltpu.SMEM((z.chunks,), jnp.int32),
            pltpu.SemaphoreType.DMA,
        ],
        compiler_params=pltpu.CompilerParams(vmem_limit_bytes=VMEM_LIMIT),
        cost_estimate=pl.CostEstimate(
            flops=1 << 33, bytes_accessed=64 << 20, transcendentals=0
        ),
        name="first_step",
    )(columns.T, stored.T, prolong_columns.T, in_hbm(stiffness), own)


def left_kernel(z, groups, table_ref, held_ref, *refs):
    terms_ref = refs[-1]
    col_pos = lax.axis_index("col")
    taken = 0
    for d, count in groups:
        left_rows(z, col_pos ^ d, refs[taken : taken + count], table_ref, held_ref, terms_ref)
        taken += count


def left_terms(z, groups, table, held, terms):
    pieces = [x for _, parts in groups for x in parts]
    n = len(groups)
    return pl.pallas_call(
        functools.partial(left_kernel, z, [(d, len(parts)) for d, parts in groups]),
        in_specs=[SMEM, VMEM] + [VMEM] * len(pieces) + [VMEM],
        out_specs=VMEM,
        out_shape=pltpu.VMEM(z.terms_shape, jnp.bfloat16),
        input_output_aliases={2 + len(pieces): 0},
        compiler_params=pltpu.CompilerParams(vmem_limit_bytes=VMEM_LIMIT),
        cost_estimate=pl.CostEstimate(
            flops=n << 32, bytes_accessed=n * (32 << 20), transcendentals=0
        ),
        name="left_terms",
    )(table, in_vmem(held), *pieces, in_vmem(terms))


def right_kernel(z, number, last, table_ref, terms_ref, *refs):
    count = len(z.batches[number])
    pieces = refs[:count]
    out_ref, right_ref, sem = refs[count + 1 :]
    acc_ref = refs[count] if last else out_ref
    copies = []
    for at, piece in enumerate(pieces):
        copy = pltpu.make_async_copy(piece, right_ref.at[pl.ds(at * z.per, z.per)], sem.at[at])
        copy.start()
        copies.append(copy)
    for copy in copies:
        copy.wait()

    def field(entry, shift):
        return lax.shift_right_logical(entry, shift) & ((1 << AGG_BITS) - 1)

    def one_unit(unit, carry):
        parts = []
        for u in range(UNIT):
            entry = table_ref[z.entry_at + unit * UNIT + u]
            row = entry & ((1 << ROW_BITS) - 1)
            right = jnp.concatenate([right_ref[row, 0], right_ref[row, 1]], axis=1)
            value = jnp.dot(terms_ref[unit * UNIT + u], right, preferred_element_type=jnp.float32)
            aggs = [field(entry, ROW_BITS + n * AGG_BITS) for n in range(4)]
            parts.append((aggs, value))
        for aggs, value in parts:
            for a in range(2):
                for b in range(2):
                    acc_ref[aggs[a] * z.agg_cols + aggs[2 + b]] += value[
                        a * z.block : (a + 1) * z.block, b * z.block : (b + 1) * z.block
                    ]
        return carry

    begin = table_ref[z.start_at + number] // UNIT
    end = table_ref[z.start_at + number + 1] // UNIT
    lax.fori_loop(begin, end, one_unit, 0)
    if last:
        copy = pltpu.make_async_copy(
            acc_ref.at[pl.ds(0, z.agg_rows * z.agg_cols)], out_ref, sem.at[0]
        )
        copy.start()
        copy.wait()


def right_sums(z, number, pieces, table, terms, acc):
    count = len(pieces)
    last = number == len(z.batches) - 1
    if last:
        out_shape = jax.ShapeDtypeStruct(
            (z.agg_rows * z.agg_cols, z.block, z.block), jnp.float32
        )
    else:
        out_shape = pltpu.VMEM(z.acc_shape, jnp.float32)
    return pl.pallas_call(
        functools.partial(right_kernel, z, number, last),
        in_specs=[SMEM, VMEM] + [HBM] * count + [VMEM],
        out_specs=HBM if last else VMEM,
        out_shape=out_shape,
        scratch_shapes=[
            pltpu.VMEM((count * z.per, 2, z.block, z.block), jnp.bfloat16),
            pltpu.SemaphoreType.DMA((count,)),
        ],
        input_output_aliases={} if last else {2 + count: 0},
        compiler_params=pltpu.CompilerParams(vmem_limit_bytes=VMEM_LIMIT),
        cost_estimate=pl.CostEstimate(
            flops=count << 32, bytes_accessed=count * (32 << 20), transcendentals=0
        ),
        name="right_sums",
    )(table, in_vmem(terms), *pieces, in_vmem(acc))


def shards(stiffness, stiff_columns, stiff_stored, prolongator, prolong_columns):
    z = Sizes(stiffness, prolongator, lax.axis_size("row"), lax.axis_size("col"))
    bar = lax.optimization_barrier

    def across(x, d):
        return lax.ppermute(x, "col", [(c, c ^ d) for c in range(z.col_count)])

    def fetch(x, m):
        pairs = [
            ((c * z.ratio + k) * z.col_count + (q ^ c ^ m), (q * z.ratio + k) * z.col_count + c)
            for q in range(z.col_count)
            for k in range(z.ratio)
            for c in range(z.col_count)
        ]
        return lax.ppermute(x, ("row", "col"), pairs)

    def beside(x, j):
        return lax.ppermute(
            x, "row", [(r, r // z.ratio * z.ratio + (r + j) % z.ratio) for r in range(z.row_count)]
        )

    near = [d for d in range(1, z.col_count) if d & (d - 1) == 0]
    held = [across(prolongator, d) for d in near]
    right = {(m, 0): fetch(prolongator, m) for m in z.early}
    table, stiff, terms, acc = first_step(
        z, stiff_columns, stiff_stored, prolong_columns, stiffness, prolongator
    )
    again, table = bar((prolongator, table))
    by = dict(zip(near, held))
    far = {}
    for d in range(1, z.col_count):
        if d in near:
            continue
        low = d & -d
        far[d] = across(by[d ^ low], low) if d ^ low in near else across(again, d)
    right |= {(m, 0): fetch(again, m) for m in z.late}
    terms = left_terms(z, [(d, [by[d]]) for d in near], table, stiff, terms)
    terms = left_terms(z, [(d, [x]) for d, x in far.items()], table, stiff, terms)
    others = range(1, z.ratio)
    right |= {(m, j): beside(right[m, 0], j) for m in z.early for j in others}
    acc = right_sums(z, 0, [right[p] for p in z.batches[0]], table, terms, acc)
    acc, *held = bar((acc, *[right[m, 0] for m in z.late]))
    right |= {(m, 0): x for m, x in zip(z.late, held)}
    right |= {(m, j): beside(right[m, 0], j) for m in z.late for j in others}
    acc = right_sums(z, 1, [right[p] for p in z.batches[1]], table, terms, acc)
    coarse = right_sums(z, 2, [right[p] for p in z.batches[2]], table, terms, acc)
    return coarse.reshape(z.agg_rows, z.agg_cols, z.block, z.block)


def solution(mesh):
    return jax.shard_map(
        shards,
        mesh=mesh,
        in_specs=(
            P("row", "col", None, None),
            P("row", "col"),
            P("row", "col"),
            P(("row", "col"), None, None, None),
            P(),
        ),
        out_specs=P("row", "col", None, None),
        check_vma=False,
    )
```

```python
import functools

import jax
import jax.numpy as jnp
from jax import lax
from jax.experimental import pallas as pl
from jax.experimental.pallas import tpu as pltpu
from jax.sharding import PartitionSpec as P

G = 8
UNIT = 16
VMEM_LIMIT = 16 << 20
HBM = pl.BlockSpec(memory_space=pltpu.HBM)
SMEM = pl.BlockSpec(memory_space=pltpu.SMEM)
VMEM = pl.BlockSpec(memory_space=pltpu.VMEM)
ROW_BITS, AGG_BITS = 8, 5


def in_vmem(x):
    return pltpu.with_memory_space_constraint(x, pltpu.VMEM)


def in_hbm(x):
    return pltpu.with_memory_space_constraint(x, pltpu.HBM)


class Sizes:
    def __init__(self, stiffness, prolongator, row_count, col_count):
        self.rows, self.slots, self.block = stiffness.shape[:3]
        self.per = prolongator.shape[0]
        self.row_count, self.col_count = row_count, col_count
        self.ratio = row_count // col_count
        self.agg_rows = self.rows // G
        self.agg_cols = self.ratio * self.agg_rows
        self.cols = self.ratio * self.rows
        self.chunks = self.cols // self.per
        self.slots_count = self.rows * self.slots
        order = [3, 0, 2, 1] if col_count == 4 else list(range(col_count))
        self.early, self.late = order[: col_count // 2], order[col_count // 2 :]
        members = range(self.ratio)
        self.arrivals = [
            [(m, j) for m in self.early for j in members],
            [(m, 0) for m in self.late],
            [(m, j) for m in self.late for j in members if j],
        ]
        self.pieces = [piece for arrival in self.arrivals for piece in arrival]
        self.batches = len(self.arrivals) + 1
        spare = self.batches * (UNIT - 1)
        self.units = -(-(self.slots_count + spare) // UNIT)
        self.entries = self.units * UNIT
        self.place_at = 0
        self.start_at = self.slots_count
        self.entry_at = self.start_at + self.batches + 1
        self.table = self.entry_at + self.entries
        self.per_bits = self.per.bit_length() - 1
        assert self.per == 1 << self.per_bits
        assert self.chunks * self.per <= 1 << ROW_BITS
        assert max(self.agg_rows, self.agg_cols) < 1 << AGG_BITS
        block = self.block
        self.terms_shape = (self.entries + 1, 2 * block, block)
        self.acc_shape = ((self.agg_rows + 1) * self.agg_cols, block, block)
        self.right_shape = (self.cols, 2, block, block)


def position(z):
    row_pos, col_pos = lax.axis_index("row"), lax.axis_index("col")
    return row_pos, col_pos, row_pos // z.ratio, row_pos % z.ratio


def list_slots(z, columns_ref, stored_ref, prolong_ref, table_ref, fill_ref, batch_ref, base_ref):
    row_pos, col_pos, range_pos, member = position(z)
    first_fine = col_pos * z.cols
    first_row = row_pos * z.rows
    first_agg = row_pos * z.agg_rows
    first_agg_col = col_pos * z.agg_cols
    right_shift = ROW_BITS + 2 * AGG_BITS
    padding = z.agg_rows * ((1 << ROW_BITS) + (1 << (ROW_BITS + AGG_BITS)))

    at = 0
    for b in range(z.batches):
        fill_ref[b] = 0
    for b, arrival in enumerate(z.arrivals):
        for m, j in arrival:
            panel = lax.rem(member - j + z.ratio, z.ratio)
            chunk = panel * z.col_count + (range_pos ^ col_pos ^ m)
            batch_ref[chunk] = b
            base_ref[chunk] = at
            at += z.per

    def batch_of(i, chunk):
        d = lax.shift_right_logical(i, z.per_bits) ^ col_pos
        b = batch_ref[chunk]
        far = jnp.logical_and((d & (d - 1)) != 0, b == 0)
        return jnp.where(far, z.batches - 1, b)

    def count(i, carry):
        for s in range(z.slots):
            chunk = lax.shift_right_logical(columns_ref[s, i] - first_fine, z.per_bits)
            b = batch_of(i, chunk)
            fill_ref[b] += jnp.where(stored_ref[s, i] != 0, 1, 0)
        return carry

    lax.fori_loop(0, z.rows, count, 0)

    at = 0
    for b in range(z.batches):
        table_ref[z.start_at + b] = at
        after = at + (fill_ref[b] + (UNIT - 1)) // UNIT * UNIT
        fill_ref[b] = at

        @pl.when(after > at)
        def _(after=after):
            for u in range(1, UNIT):
                table_ref[z.entry_at + after - u] = padding

        at = after
    table_ref[z.start_at + z.batches] = at

    def place(i, carry):
        first = prolong_ref[0, first_row + i] - first_agg
        second = prolong_ref[1, first_row + i] - first_agg
        left = first * (1 << ROW_BITS) + second * (1 << (ROW_BITS + AGG_BITS))
        for s in range(z.slots):
            column = columns_ref[s, i]
            col = column - first_fine
            chunk = lax.shift_right_logical(col, z.per_bits)
            b = batch_of(i, chunk)
            row = base_ref[chunk] + (col & (z.per - 1))
            right = (prolong_ref[0, column] - first_agg_col) * (1 << right_shift)
            right += (prolong_ref[1, column] - first_agg_col) * (1 << (right_shift + AGG_BITS))
            stored = stored_ref[s, i] != 0
            at = fill_ref[b]
            table_ref[z.place_at + i * z.slots + s] = jnp.where(stored, at, z.entries)

            @pl.when(stored)
            def _(b=b, at=at, entry=row + left + right):
                table_ref[z.entry_at + at] = entry
                fill_ref[b] = at + 1

        return carry

    lax.fori_loop(0, z.rows, place, 0)


def left_rows(z, chunk, parts, table_ref, stiff_ref, terms_ref):
    first = chunk * z.per
    row = 0
    for piece in parts:
        for j in range(piece.shape[0]):
            left = jnp.concatenate([piece[j, 0].T, piece[j, 1].T], axis=0)
            for s in range(0, z.slots, 2):
                pair = range(s, min(s + 2, z.slots))
                right = jnp.concatenate([stiff_ref[first + row, t] for t in pair], axis=1)
                terms = jnp.dot(left, right, preferred_element_type=jnp.float32)
                for at, t in enumerate(pair):
                    place = table_ref[z.place_at + (first + row) * z.slots + t]
                    terms_ref[place] = terms[:, at * z.block : (at + 1) * z.block].astype(
                        jnp.bfloat16
                    )
            row += 1


def first_kernel(z, columns_ref, stored_ref, prolong_ref, stiff_ref, own_ref, *refs):
    table_ref, held_ref, terms_ref, acc_ref, _, *scratch, sem = refs
    col_pos = lax.axis_index("col")
    load = pltpu.make_async_copy(stiff_ref, held_ref, sem)
    load.start()
    list_slots(z, columns_ref, stored_ref, prolong_ref, table_ref, *scratch)
    acc_ref[...] = jnp.zeros_like(acc_ref)
    load.wait()
    left_rows(z, col_pos, [own_ref], table_ref, held_ref, terms_ref)


def first_step(z, columns, stored, prolong_columns, stiffness, own):
    return pl.pallas_call(
        functools.partial(first_kernel, z),
        in_specs=[SMEM] * 3 + [HBM, VMEM],
        out_specs=[SMEM, VMEM, VMEM, VMEM, VMEM],
        out_shape=[
            jax.ShapeDtypeStruct((z.table,), jnp.int32),
            pltpu.VMEM(stiffness.shape, stiffness.dtype),
            pltpu.VMEM(z.terms_shape, jnp.bfloat16),
            pltpu.VMEM(z.acc_shape, jnp.float32),
            pltpu.VMEM(z.right_shape, jnp.bfloat16),
        ],
        scratch_shapes=[
            pltpu.SMEM((z.batches,), jnp.int32),
            pltpu.SMEM((z.chunks,), jnp.int32),
            pltpu.SMEM((z.chunks,), jnp.int32),
            pltpu.SemaphoreType.DMA,
        ],
        compiler_params=pltpu.CompilerParams(vmem_limit_bytes=VMEM_LIMIT),
        cost_estimate=pl.CostEstimate(
            flops=1 << 33, bytes_accessed=64 << 20, transcendentals=0
        ),
        name="first_step",
    )(columns.T, stored.T, prolong_columns.T, in_hbm(stiffness), own)


def left_kernel(z, groups, table_ref, held_ref, *refs):
    terms_ref = refs[-1]
    col_pos = lax.axis_index("col")
    taken = 0
    for d, count in groups:
        left_rows(z, col_pos ^ d, refs[taken : taken + count], table_ref, held_ref, terms_ref)
        taken += count


def left_terms(z, groups, table, held, terms):
    pieces = [x for _, parts in groups for x in parts]
    n = len(groups)
    return pl.pallas_call(
        functools.partial(left_kernel, z, [(d, len(parts)) for d, parts in groups]),
        in_specs=[SMEM, VMEM] + [VMEM] * len(pieces) + [VMEM],
        out_specs=VMEM,
        out_shape=pltpu.VMEM(z.terms_shape, jnp.bfloat16),
        input_output_aliases={2 + len(pieces): 0},
        compiler_params=pltpu.CompilerParams(vmem_limit_bytes=VMEM_LIMIT),
        cost_estimate=pl.CostEstimate(
            flops=n << 32, bytes_accessed=n * (32 << 20), transcendentals=0
        ),
        name="left_terms",
    )(table, in_vmem(held), *pieces, in_vmem(terms))


def add_batch(z, number, table_ref, terms_ref, right_ref, acc_ref, base=0):
    def field(entry, shift):
        return lax.shift_right_logical(entry, shift) & ((1 << AGG_BITS) - 1)

    def one_unit(unit, carry):
        parts = []
        for u in range(UNIT):
            entry = table_ref[z.entry_at + unit * UNIT + u]
            row = jnp.maximum((entry & ((1 << ROW_BITS) - 1)) - base, 0)
            left = terms_ref[unit * UNIT + u]
            value = [
                jnp.dot(left, right_ref[row, b], preferred_element_type=jnp.float32)
                for b in range(2)
            ]
            aggs = [field(entry, ROW_BITS + n * AGG_BITS) for n in range(4)]
            parts.append((aggs, value))
        for aggs, value in parts:
            for a in range(2):
                for b in range(2):
                    acc_ref[aggs[a] * z.agg_cols + aggs[2 + b]] += value[b][
                        a * z.block : (a + 1) * z.block
                    ]
        return carry

    begin = lax.shift_right_logical(table_ref[z.start_at + number], UNIT.bit_length() - 1)
    end = lax.shift_right_logical(table_ref[z.start_at + number + 1], UNIT.bit_length() - 1)
    lax.fori_loop(begin, end, one_unit, 0)


def right_kernel(z, number, table_ref, terms_ref, *refs):
    pieces = z.arrivals[number]
    first = z.pieces.index(pieces[0])
    right_ref, acc_ref, sem = refs[len(pieces) + 2 :]
    copies = []
    for at, piece in enumerate(refs[: len(pieces)]):
        place = right_ref.at[pl.ds((first + at) * z.per, z.per)]
        copy = pltpu.make_async_copy(piece, place, sem.at[at])
        copy.start()
        copies.append(copy)
    for copy in copies:
        copy.wait()
    add_batch(z, number, table_ref, terms_ref, right_ref, acc_ref)


def right_sums(z, number, pieces, table, terms, right, acc):
    count = len(pieces)
    return pl.pallas_call(
        functools.partial(right_kernel, z, number),
        in_specs=[SMEM, VMEM] + [HBM] * count + [VMEM] * 2,
        out_specs=[VMEM] * 2,
        out_shape=[pltpu.VMEM(z.right_shape, jnp.bfloat16), pltpu.VMEM(z.acc_shape, jnp.float32)],
        scratch_shapes=[pltpu.SemaphoreType.DMA((count,))],
        input_output_aliases={2 + count: 0, 3 + count: 1},
        compiler_params=pltpu.CompilerParams(vmem_limit_bytes=VMEM_LIMIT),
        cost_estimate=pl.CostEstimate(
            flops=count << 32, bytes_accessed=count * (32 << 20), transcendentals=0
        ),
        name="right_sums",
    )(table, in_vmem(terms), *pieces, in_vmem(right), in_vmem(acc))


def far_kernel(z, groups, table_ref, held_ref, *refs):
    right_ref = refs[len(groups)]
    terms_ref, acc_ref = refs[-2:]
    col_pos = lax.axis_index("col")
    for d, piece in zip(groups, refs):
        left_rows(z, col_pos ^ d, [piece], table_ref, held_ref, terms_ref)
    add_batch(z, z.batches - 1, table_ref, terms_ref, right_ref, acc_ref)


def far_step(z, groups, pieces, table, held, right, terms, acc):
    count = len(pieces)
    return pl.pallas_call(
        functools.partial(far_kernel, z, groups),
        in_specs=[SMEM, VMEM] + [VMEM] * count + [VMEM] * 3,
        out_specs=[VMEM] * 2,
        out_shape=[pltpu.VMEM(z.terms_shape, jnp.bfloat16), pltpu.VMEM(z.acc_shape, jnp.float32)],
        input_output_aliases={3 + count: 0, 4 + count: 1},
        compiler_params=pltpu.CompilerParams(vmem_limit_bytes=VMEM_LIMIT),
        cost_estimate=pl.CostEstimate(
            flops=count << 32, bytes_accessed=count * (32 << 20), transcendentals=0
        ),
        name="far_step",
    )(table, in_vmem(held), *pieces, in_vmem(right), in_vmem(terms), in_vmem(acc))


def last_kernel(z, number, table_ref, terms_ref, *refs):
    pieces = z.arrivals[number]
    acc_ref, out_ref, right_ref, sem = refs[len(pieces) :]
    base = z.pieces.index(pieces[0])
    copies = []
    for at, piece in enumerate(refs[: len(pieces)]):
        place = right_ref.at[pl.ds(at * z.per, z.per)]
        copies.append(pltpu.make_async_copy(piece, place, sem.at[at]))
        copies[-1].start()
    for copy in copies:
        copy.wait()
    add_batch(z, number, table_ref, terms_ref, right_ref, acc_ref, base * z.per)
    copy = pltpu.make_async_copy(
        acc_ref.at[pl.ds(0, z.agg_rows * z.agg_cols)], out_ref, sem.at[0]
    )
    copy.start()
    copy.wait()


def last_step(z, number, pieces, table, terms, acc):
    count = len(pieces)
    return pl.pallas_call(
        functools.partial(last_kernel, z, number),
        in_specs=[SMEM, VMEM] + [HBM] * count + [VMEM],
        out_specs=HBM,
        out_shape=jax.ShapeDtypeStruct(
            (z.agg_rows * z.agg_cols, z.block, z.block), jnp.float32
        ),
        scratch_shapes=[
            pltpu.VMEM((count * z.per, 2, z.block, z.block), jnp.bfloat16),
            pltpu.SemaphoreType.DMA((count,)),
        ],
        compiler_params=pltpu.CompilerParams(vmem_limit_bytes=VMEM_LIMIT),
        cost_estimate=pl.CostEstimate(
            flops=count << 32, bytes_accessed=count * (32 << 20), transcendentals=0
        ),
        name="last_step",
    )(table, in_vmem(terms), *pieces, in_vmem(acc))


def shards(stiffness, stiff_columns, stiff_stored, prolongator, prolong_columns):
    z = Sizes(stiffness, prolongator, lax.axis_size("row"), lax.axis_size("col"))
    bar = lax.optimization_barrier

    def across(x, d):
        return lax.ppermute(x, "col", [(c, c ^ d) for c in range(z.col_count)])

    def fetch(x, m):
        pairs = [
            ((c * z.ratio + k) * z.col_count + (q ^ c ^ m), (q * z.ratio + k) * z.col_count + c)
            for q in range(z.col_count)
            for k in range(z.ratio)
            for c in range(z.col_count)
        ]
        return lax.ppermute(x, ("row", "col"), pairs)

    def beside(x, j):
        return lax.ppermute(
            x, "row", [(r, r // z.ratio * z.ratio + (r + j) % z.ratio) for r in range(z.row_count)]
        )

    near = [d for d in range(1, z.col_count) if d & (d - 1) == 0]
    held = [across(prolongator, d) for d in near]
    right = {(m, 0): fetch(prolongator, m) for m in z.early}
    table, stiff, terms, acc, panel = first_step(
        z, stiff_columns, stiff_stored, prolong_columns, stiffness, prolongator
    )
    again, table = bar((prolongator, table))
    table, *held = bar((table, *held))
    by = dict(zip(near, held))
    far = {}
    for d in range(1, z.col_count):
        if d in near:
            continue
        low = d & -d
        far[d] = across(by[d ^ low], low) if d ^ low in near else across(again, d)
    right |= {(m, 0): fetch(again, m) for m in z.late}
    terms = left_terms(z, [(d, [by[d]]) for d in near], table, stiff, terms)
    others = range(1, z.ratio)
    right |= {(m, j): beside(right[m, 0], j) for m in z.early for j in others}

    def add(number, panel, acc):
        return right_sums(
            z, number, [right[p] for p in z.arrivals[number]], table, terms, panel, acc
        )

    panel, acc = add(0, panel, acc)
    terms, acc = far_step(z, list(far), list(far.values()), table, stiff, panel, terms, acc)
    acc, *held = bar((acc, *[right[m, 0] for m in z.late]))
    right |= {(m, 0): x for m, x in zip(z.late, held)}
    right |= {(m, j): beside(right[m, 0], j) for m in z.late for j in others}
    panel, acc = add(1, panel, acc)
    coarse = last_step(z, 2, [right[p] for p in z.arrivals[2]], table, terms, acc)
    return coarse.reshape(z.agg_rows, z.agg_cols, z.block, z.block)


def solution(mesh):
    return jax.shard_map(
        shards,
        mesh=mesh,
        in_specs=(
            P("row", "col", None, None),
            P("row", "col"),
            P("row", "col"),
            P(("row", "col"), None, None, None),
            P(),
        ),
        out_specs=P("row", "col", None, None),
        check_vma=False,
    )
```

```python
import functools

import jax
import jax.numpy as jnp
from jax import lax
from jax.experimental import pallas as pl
from jax.experimental.pallas import tpu as pltpu
from jax.sharding import PartitionSpec as P

G = 8
UNIT = 16
VMEM_LIMIT = 16 << 20
HBM = pl.BlockSpec(memory_space=pltpu.HBM)
SMEM = pl.BlockSpec(memory_space=pltpu.SMEM)
VMEM = pl.BlockSpec(memory_space=pltpu.VMEM)
ROW_BITS, AGG_BITS = 8, 5


def in_vmem(x):
    return pltpu.with_memory_space_constraint(x, pltpu.VMEM)


def in_hbm(x):
    return pltpu.with_memory_space_constraint(x, pltpu.HBM)


class Sizes:
    def __init__(self, stiffness, prolongator, row_count, col_count):
        self.rows, self.slots, self.block = stiffness.shape[:3]
        self.per = prolongator.shape[0]
        self.row_count, self.col_count = row_count, col_count
        self.ratio = row_count // col_count
        self.agg_rows = self.rows // G
        self.agg_cols = self.ratio * self.agg_rows
        self.cols = self.ratio * self.rows
        self.chunks = self.cols // self.per
        self.slots_count = self.rows * self.slots
        order = [3, 0, 2, 1] if col_count == 4 else list(range(col_count))
        self.early, self.late = order[: col_count // 2], order[col_count // 2 :]
        members = range(self.ratio)
        self.arrivals = [
            [(m, j) for m in self.early for j in members],
            [(m, 0) for m in self.late],
            [(m, j) for m in self.late for j in members if j],
        ]
        self.pieces = [piece for arrival in self.arrivals for piece in arrival]
        self.batches = len(self.arrivals) + 1
        spare = self.batches * (UNIT - 1)
        self.units = -(-(self.slots_count + spare) // UNIT)
        self.entries = self.units * UNIT
        self.place_at = 0
        self.start_at = self.slots_count
        self.entry_at = self.start_at + self.batches + 1
        self.table = self.entry_at + self.entries
        self.per_bits = self.per.bit_length() - 1
        assert self.per == 1 << self.per_bits
        assert self.chunks * self.per <= 1 << ROW_BITS
        assert max(self.agg_rows, self.agg_cols) < 1 << AGG_BITS
        block = self.block
        self.terms_shape = (self.entries + 1, 2 * block, block)
        self.acc_shape = ((self.agg_rows + 1) * self.agg_cols, block, block)
        self.right_shape = (self.cols, 2, block, block)


def position(z):
    row_pos, col_pos = lax.axis_index("row"), lax.axis_index("col")
    return row_pos, col_pos, row_pos // z.ratio, row_pos % z.ratio


def list_slots(z, columns_ref, stored_ref, prolong_ref, table_ref, fill_ref, batch_ref, base_ref):
    row_pos, col_pos, range_pos, member = position(z)
    first_fine = col_pos * z.cols
    first_row = row_pos * z.rows
    first_agg = row_pos * z.agg_rows
    first_agg_col = col_pos * z.agg_cols
    right_shift = ROW_BITS + 2 * AGG_BITS
    padding = z.agg_rows * ((1 << ROW_BITS) + (1 << (ROW_BITS + AGG_BITS)))

    at = 0
    for b in range(z.batches):
        fill_ref[b] = 0
    for b, arrival in enumerate(z.arrivals):
        for m, j in arrival:
            panel = lax.rem(member - j + z.ratio, z.ratio)
            chunk = panel * z.col_count + (range_pos ^ col_pos ^ m)
            batch_ref[chunk] = b
            base_ref[chunk] = at
            at += z.per

    def batch_of(i, chunk):
        d = lax.shift_right_logical(i, z.per_bits) ^ col_pos
        b = batch_ref[chunk]
        far = jnp.logical_and((d & (d - 1)) != 0, b == 0)
        return jnp.where(far, z.batches - 1, b)

    def count(i, carry):
        for s in range(z.slots):
            chunk = lax.shift_right_logical(columns_ref[s, i] - first_fine, z.per_bits)
            b = batch_of(i, chunk)
            fill_ref[b] += jnp.where(stored_ref[s, i] != 0, 1, 0)
        return carry

    lax.fori_loop(0, z.rows, count, 0)

    at = 0
    for b in range(z.batches):
        table_ref[z.start_at + b] = at
        after = at + (fill_ref[b] + (UNIT - 1)) // UNIT * UNIT
        fill_ref[b] = at

        @pl.when(after > at)
        def _(after=after):
            for u in range(1, UNIT):
                table_ref[z.entry_at + after - u] = padding

        at = after
    table_ref[z.start_at + z.batches] = at

    def place(i, carry):
        first = prolong_ref[0, first_row + i] - first_agg
        second = prolong_ref[1, first_row + i] - first_agg
        left = first * (1 << ROW_BITS) + second * (1 << (ROW_BITS + AGG_BITS))
        for s in range(z.slots):
            column = columns_ref[s, i]
            col = column - first_fine
            chunk = lax.shift_right_logical(col, z.per_bits)
            b = batch_of(i, chunk)
            row = base_ref[chunk] + (col & (z.per - 1))
            right = (prolong_ref[0, column] - first_agg_col) * (1 << right_shift)
            right += (prolong_ref[1, column] - first_agg_col) * (1 << (right_shift + AGG_BITS))
            stored = stored_ref[s, i] != 0
            at = fill_ref[b]
            table_ref[z.place_at + i * z.slots + s] = jnp.where(stored, at, z.entries)

            @pl.when(stored)
            def _(b=b, at=at, entry=row + left + right):
                table_ref[z.entry_at + at] = entry
                fill_ref[b] = at + 1

        return carry

    lax.fori_loop(0, z.rows, place, 0)


def left_rows(z, chunk, parts, table_ref, stiff_ref, terms_ref):
    first = chunk * z.per
    row = 0
    for piece in parts:
        for j in range(piece.shape[0]):
            left = jnp.concatenate([piece[j, 0].T, piece[j, 1].T], axis=0)
            for s in range(0, z.slots, 2):
                pair = range(s, min(s + 2, z.slots))
                right = jnp.concatenate([stiff_ref[first + row, t] for t in pair], axis=1)
                terms = jnp.dot(left, right, preferred_element_type=jnp.float32)
                for at, t in enumerate(pair):
                    place = table_ref[z.place_at + (first + row) * z.slots + t]
                    terms_ref[place] = terms[:, at * z.block : (at + 1) * z.block].astype(
                        jnp.bfloat16
                    )
            row += 1


def first_kernel(z, columns_ref, stored_ref, prolong_ref, stiff_ref, own_ref, *refs):
    table_ref, held_ref, terms_ref, acc_ref, _, *scratch, sem = refs
    col_pos = lax.axis_index("col")
    load = pltpu.make_async_copy(stiff_ref, held_ref, sem)
    load.start()
    list_slots(z, columns_ref, stored_ref, prolong_ref, table_ref, *scratch)
    acc_ref[...] = jnp.zeros_like(acc_ref)
    terms_ref[...] = jnp.zeros_like(terms_ref)
    load.wait()
    left_rows(z, col_pos, [own_ref], table_ref, held_ref, terms_ref)


def first_step(z, columns, stored, prolong_columns, stiffness, own):
    return pl.pallas_call(
        functools.partial(first_kernel, z),
        in_specs=[SMEM] * 3 + [HBM, VMEM],
        out_specs=[SMEM, VMEM, VMEM, VMEM, VMEM],
        out_shape=[
            jax.ShapeDtypeStruct((z.table,), jnp.int32),
            pltpu.VMEM(stiffness.shape, stiffness.dtype),
            pltpu.VMEM(z.terms_shape, jnp.bfloat16),
            pltpu.VMEM(z.acc_shape, jnp.float32),
            pltpu.VMEM(z.right_shape, jnp.bfloat16),
        ],
        scratch_shapes=[
            pltpu.SMEM((z.batches,), jnp.int32),
            pltpu.SMEM((z.chunks,), jnp.int32),
            pltpu.SMEM((z.chunks,), jnp.int32),
            pltpu.SemaphoreType.DMA,
        ],
        compiler_params=pltpu.CompilerParams(vmem_limit_bytes=VMEM_LIMIT),
        cost_estimate=pl.CostEstimate(
            flops=1 << 33, bytes_accessed=64 << 20, transcendentals=0
        ),
        name="first_step",
    )(columns.T, stored.T, prolong_columns.T, in_hbm(stiffness), own)


def left_kernel(z, groups, table_ref, held_ref, *refs):
    terms_ref = refs[-1]
    col_pos = lax.axis_index("col")
    taken = 0
    for d, count in groups:
        left_rows(z, col_pos ^ d, refs[taken : taken + count], table_ref, held_ref, terms_ref)
        taken += count


def left_terms(z, groups, table, held, terms):
    pieces = [x for _, parts in groups for x in parts]
    n = len(groups)
    return pl.pallas_call(
        functools.partial(left_kernel, z, [(d, len(parts)) for d, parts in groups]),
        in_specs=[SMEM, VMEM] + [VMEM] * len(pieces) + [VMEM],
        out_specs=VMEM,
        out_shape=pltpu.VMEM(z.terms_shape, jnp.bfloat16),
        input_output_aliases={2 + len(pieces): 0},
        compiler_params=pltpu.CompilerParams(vmem_limit_bytes=VMEM_LIMIT),
        cost_estimate=pl.CostEstimate(
            flops=n << 32, bytes_accessed=n * (32 << 20), transcendentals=0
        ),
        name="left_terms",
    )(table, in_vmem(held), *pieces, in_vmem(terms))


def add_batch(z, number, table_ref, terms_ref, right_ref, acc_ref, base=0):
    def field(entry, shift):
        return lax.shift_right_logical(entry, shift) & ((1 << AGG_BITS) - 1)

    def one_unit(unit, carry):
        parts = []
        for u in range(UNIT):
            entry = table_ref[z.entry_at + unit * UNIT + u]
            row = jnp.maximum((entry & ((1 << ROW_BITS) - 1)) - base, 0)
            left = terms_ref[unit * UNIT + u]
            value = [
                jnp.dot(left, right_ref[row, b], preferred_element_type=jnp.float32)
                for b in range(2)
            ]
            aggs = [field(entry, ROW_BITS + n * AGG_BITS) for n in range(4)]
            parts.append((aggs, value))
        for aggs, value in parts:
            for a in range(2):
                for b in range(2):
                    acc_ref[aggs[a] * z.agg_cols + aggs[2 + b]] += value[b][
                        a * z.block : (a + 1) * z.block
                    ]
        return carry

    begin = lax.shift_right_logical(table_ref[z.start_at + number], UNIT.bit_length() - 1)
    end = lax.shift_right_logical(table_ref[z.start_at + number + 1], UNIT.bit_length() - 1)
    lax.fori_loop(begin, end, one_unit, 0)


def right_kernel(z, number, table_ref, terms_ref, *refs):
    pieces = z.arrivals[number]
    first = z.pieces.index(pieces[0])
    right_ref, acc_ref, sem = refs[len(pieces) + 2 :]
    copies = []
    for at, piece in enumerate(refs[: len(pieces)]):
        place = right_ref.at[pl.ds((first + at) * z.per, z.per)]
        copy = pltpu.make_async_copy(piece, place, sem.at[at])
        copy.start()
        copies.append(copy)
    for copy in copies:
        copy.wait()
    add_batch(z, number, table_ref, terms_ref, right_ref, acc_ref)


def right_sums(z, number, pieces, table, terms, right, acc):
    count = len(pieces)
    return pl.pallas_call(
        functools.partial(right_kernel, z, number),
        in_specs=[SMEM, VMEM] + [HBM] * count + [VMEM] * 2,
        out_specs=[VMEM] * 2,
        out_shape=[pltpu.VMEM(z.right_shape, jnp.bfloat16), pltpu.VMEM(z.acc_shape, jnp.float32)],
        scratch_shapes=[pltpu.SemaphoreType.DMA((count,))],
        input_output_aliases={2 + count: 0, 3 + count: 1},
        compiler_params=pltpu.CompilerParams(vmem_limit_bytes=VMEM_LIMIT),
        cost_estimate=pl.CostEstimate(
            flops=count << 32, bytes_accessed=count * (32 << 20), transcendentals=0
        ),
        name="right_sums",
    )(table, in_vmem(terms), *pieces, in_vmem(right), in_vmem(acc))


def far_kernel(z, groups, table_ref, held_ref, *refs):
    right_ref = refs[len(groups)]
    terms_ref, acc_ref = refs[-2:]
    col_pos = lax.axis_index("col")
    for d, piece in zip(groups, refs):
        left_rows(z, col_pos ^ d, [piece], table_ref, held_ref, terms_ref)
    add_batch(z, z.batches - 1, table_ref, terms_ref, right_ref, acc_ref)


def far_step(z, groups, pieces, table, held, right, terms, acc):
    count = len(pieces)
    return pl.pallas_call(
        functools.partial(far_kernel, z, groups),
        in_specs=[SMEM, VMEM] + [VMEM] * count + [VMEM] * 3,
        out_specs=[VMEM] * 2,
        out_shape=[pltpu.VMEM(z.terms_shape, jnp.bfloat16), pltpu.VMEM(z.acc_shape, jnp.float32)],
        input_output_aliases={3 + count: 0, 4 + count: 1},
        compiler_params=pltpu.CompilerParams(vmem_limit_bytes=VMEM_LIMIT),
        cost_estimate=pl.CostEstimate(
            flops=count << 32, bytes_accessed=count * (32 << 20), transcendentals=0
        ),
        name="far_step",
    )(table, in_vmem(held), *pieces, in_vmem(right), in_vmem(terms), in_vmem(acc))


def last_kernel(z, number, table_ref, terms_ref, *refs):
    pieces = z.arrivals[number]
    acc_ref, out_ref, right_ref, sem = refs[len(pieces) :]
    base = z.pieces.index(pieces[0])
    copies = []
    for at, piece in enumerate(refs[: len(pieces)]):
        place = right_ref.at[pl.ds(at * z.per, z.per)]
        copies.append(pltpu.make_async_copy(piece, place, sem.at[at]))
        copies[-1].start()
    for copy in copies:
        copy.wait()
    add_batch(z, number, table_ref, terms_ref, right_ref, acc_ref, base * z.per)
    copy = pltpu.make_async_copy(
        acc_ref.at[pl.ds(0, z.agg_rows * z.agg_cols)], out_ref, sem.at[0]
    )
    copy.start()
    copy.wait()


def last_step(z, number, pieces, table, terms, acc):
    count = len(pieces)
    return pl.pallas_call(
        functools.partial(last_kernel, z, number),
        in_specs=[SMEM, VMEM] + [HBM] * count + [VMEM],
        out_specs=HBM,
        out_shape=jax.ShapeDtypeStruct(
            (z.agg_rows * z.agg_cols, z.block, z.block), jnp.float32
        ),
        scratch_shapes=[
            pltpu.VMEM((count * z.per, 2, z.block, z.block), jnp.bfloat16),
            pltpu.SemaphoreType.DMA((count,)),
        ],
        compiler_params=pltpu.CompilerParams(vmem_limit_bytes=VMEM_LIMIT),
        cost_estimate=pl.CostEstimate(
            flops=count << 32, bytes_accessed=count * (32 << 20), transcendentals=0
        ),
        name="last_step",
    )(table, in_vmem(terms), *pieces, in_vmem(acc))


def shards(stiffness, stiff_columns, stiff_stored, prolongator, prolong_columns):
    z = Sizes(stiffness, prolongator, lax.axis_size("row"), lax.axis_size("col"))
    bar = lax.optimization_barrier

    def across(x, d):
        return lax.ppermute(x, "col", [(c, c ^ d) for c in range(z.col_count)])

    def fetch(x, m):
        pairs = [
            ((c * z.ratio + k) * z.col_count + (q ^ c ^ m), (q * z.ratio + k) * z.col_count + c)
            for q in range(z.col_count)
            for k in range(z.ratio)
            for c in range(z.col_count)
        ]
        return lax.ppermute(x, ("row", "col"), pairs)

    def beside(x, j):
        return lax.ppermute(
            x, "row", [(r, r // z.ratio * z.ratio + (r + j) % z.ratio) for r in range(z.row_count)]
        )

    near = [d for d in range(1, z.col_count) if d & (d - 1) == 0]
    held = [across(prolongator, d) for d in near]
    right = {(m, 0): fetch(prolongator, m) for m in z.early}
    table, stiff, terms, acc, panel = first_step(
        z, stiff_columns, stiff_stored, prolong_columns, stiffness, prolongator
    )
    again, table = bar((prolongator, table))
    table, *held = bar((table, *held))
    by = dict(zip(near, held))
    far = {}
    for d in range(1, z.col_count):
        if d in near:
            continue
        low = d & -d
        far[d] = across(by[d ^ low], low) if d ^ low in near else across(again, d)
    right |= {(m, 0): fetch(again, m) for m in z.late}
    terms = left_terms(z, [(d, [by[d]]) for d in near], table, stiff, terms)
    others = range(1, z.ratio)
    right |= {(m, j): beside(right[m, 0], j) for m in z.early for j in others}

    def add(number, panel, acc):
        return right_sums(
            z, number, [right[p] for p in z.arrivals[number]], table, terms, panel, acc
        )

    panel, acc = add(0, panel, acc)
    terms, acc = far_step(z, list(far), list(far.values()), table, stiff, panel, terms, acc)
    acc, *held = bar((acc, *[right[m, 0] for m in z.late]))
    right |= {(m, 0): x for m, x in zip(z.late, held)}
    right |= {(m, j): beside(right[m, 0], j) for m in z.late for j in others}
    panel, acc = add(1, panel, acc)
    coarse = last_step(z, 2, [right[p] for p in z.arrivals[2]], table, terms, acc)
    return coarse.reshape(z.agg_rows, z.agg_cols, z.block, z.block)


def solution(mesh):
    return jax.shard_map(
        shards,
        mesh=mesh,
        in_specs=(
            P("row", "col", None, None),
            P("row", "col"),
            P("row", "col"),
            P(("row", "col"), None, None, None),
            P(),
        ),
        out_specs=P("row", "col", None, None),
        check_vma=False,
    )
```
